32 devices in a mesh: tm: 4 (over y, x), dp: 8 (over z, core).
Axes of the slice: x: 2, y: 2, z: 4, core: 2. Of those that a mesh axis runs over, the one named last changes fastest.
Arguments:
- features: bfloat16 [8, 8, 16, 24, 384], P('dp', 'tm'), may hold values from -60 to 60
- conv_weight: bfloat16 [10368, 384], replicated, may hold values from -0.0625 to 0.0625
- up_weight: bfloat16 [1152, 768], replicated, may hold values from -0.1875 to 0.1875
- cotangent: bfloat16 [8, 16, 16, 24, 384], P('dp', 'tm'), may hold values from -6 to 6
Outputs:
- features_grad: bfloat16 [8, 8, 16, 24, 384], P('dp', 'tm')
- grad_conv: float32 [10368, 384], P('dp', 'tm')
- grad_up: float32 [1152, 768], P('dp', 'tm')
The draws below stay inside these ranges and needn't reach their ends.
All inputs are finite; a program needn't handle non-finite values.
Results may differ from the reference program's by a relative error of at most 0.0049.
Values may be sent and summed in bfloat16 or wider, within the bound.
A program may use at most 128 MiB of HBM per device.

```python
import math
import jax
import jax.numpy as jnp
from jax import lax

C = 384
G = 32
HT = 16
WD = 24
CROPS = 8
LFRAMES = 8
POSITIONS = 24576


def draw_features(key, part):
    first, second, third = jax.random.split(key, 3)
    shape = (CROPS, LFRAMES, HT, WD, C)
    base = jnp.clip(jax.random.normal(first, shape, jnp.float32), -6.0, 6.0)
    pixel = jnp.exp(jax.random.uniform(second, (CROPS, LFRAMES, HT, WD, 1), jnp.float32, 0.0, 2.3))
    channel = jnp.exp(jax.random.uniform(third, (C,), jnp.float32, 0.0, 2.3))
    return (base * pixel * channel * 0.1).astype(jnp.bfloat16)


def level_of(own_key, extent, pieces, smallest, largest):
    gain, own = 1.0, jax.random.fold_in(own_key, 6)
    for axis_at, blocks in pieces:
        heights = jnp.exp(jax.random.uniform(jax.random.fold_in(own, axis_at), (blocks,), jnp.float32, smallest / len(pieces), largest / len(pieces)))
        gain = gain * jnp.repeat(heights, extent[axis_at] // blocks).reshape([-1 if axis == axis_at else 1 for axis in range(len(extent))])
    return gain


def centred(key, shape, scale, limit, pieces=(), kind=jnp.bfloat16):
    values = scale * jax.random.normal(key, shape, jnp.float32)
    if pieces:
        values = values * level_of(key, shape, pieces, -0.22, 0.18)
    return jnp.clip(values, -limit, limit).astype(kind)


def setup_inputs(seed: int = 0) -> dict:
    key_list = jax.random.split(jax.random.key(seed), 5)
    return {
        "features": draw_features(jax.random.fold_in(key_list[4], 71), 0),
        "conv_weight": centred(key_list[1], (27 * C, C), (27 * C) ** -0.5, 0.0625),
        "up_weight": centred(key_list[2], (3 * C, 2 * C), (3 * C) ** -0.5, 0.1875),
        "cotangent": centred(key_list[3], (CROPS, 2 * LFRAMES, HT, WD, C), 1.0, 6.0, ((0, 8), (1, 4))),
    }


EPSILON = 1e-06

def norm_act(field):
    shape = field.shape
    grouped = field.reshape(shape[:-3] + (shape[-3] * shape[-2], G, shape[-1] // G))
    center = grouped - lax.optimization_barrier(jnp.mean(grouped, axis=(-3, -1), keepdims=True))
    spread = lax.optimization_barrier(jnp.mean(center * center, axis=(-3, -1), keepdims=True))
    normed = center * lax.rsqrt(spread + EPSILON)
    return jax.nn.silu(normed).reshape(shape)

def reference(features, conv_weight, up_weight, cotangent):
    kernel = conv_weight.reshape(3, 3, 3, C, C)
    up_kernel = up_weight.reshape(3, C, 2 * C)

    def per_crop(totals, inputs):
        clip, clip_grad = inputs
        field = clip.astype(jnp.float32)
        act_float, pullback = jax.vjp(norm_act, field)
        act = act_float.astype(jnp.bfloat16)
        act_pad = jnp.pad(act, ((2, 0), (1, 1), (1, 1), (0, 0)))
        conv_out = jnp.zeros((LFRAMES * HT * WD, C), jnp.float32)
        for time_tap in range(3):
            for high_tap in range(3):
                for wide_tap in range(3):
                    window = act_pad[time_tap:time_tap + LFRAMES, high_tap:high_tap + HT, wide_tap:wide_tap + WD].reshape(-1, C)
                    conv_out = conv_out + jnp.dot(window, kernel[time_tap, high_tap, wide_tap], preferred_element_type=jnp.float32)
        hidden = (field.reshape(-1, C) + conv_out).astype(jnp.bfloat16).reshape(LFRAMES, HT, WD, C)
        up_grad = clip_grad.reshape(LFRAMES, 2, HT, WD, C).transpose(0, 2, 3, 1, 4).reshape(LFRAMES, HT, WD, 2 * C)
        hidden_pad = jnp.pad(hidden, ((2, 0), (0, 0), (0, 0), (0, 0)))
        up_pad = jnp.pad(up_grad, ((0, 2), (0, 0), (0, 0), (0, 0)))
        up_flat = up_grad.reshape(-1, 2 * C)
        hidden_grad = jnp.zeros((LFRAMES * HT * WD, C), jnp.float32)
        up_terms = []
        for tap in range(3):
            hidden_grad = hidden_grad + jnp.dot(up_pad[tap:tap + LFRAMES].reshape(-1, 2 * C), up_kernel[2 - tap].T, preferred_element_type=jnp.float32)
            up_terms.append(jnp.dot(hidden_pad[tap:tap + LFRAMES].reshape(-1, C).T, up_flat, preferred_element_type=jnp.float32))
        conv_grad = hidden_grad.astype(jnp.bfloat16)
        grad_pad = jnp.pad(conv_grad.reshape(LFRAMES, HT, WD, C), ((0, 2), (1, 1), (1, 1), (0, 0)))
        act_grad = jnp.zeros((LFRAMES * HT * WD, C), jnp.float32)
        conv_terms = []
        for time_tap in range(3):
            for high_tap in range(3):
                for wide_tap in range(3):
                    later = grad_pad[2 - time_tap:2 - time_tap + LFRAMES, 2 - high_tap:2 - high_tap + HT, 2 - wide_tap:2 - wide_tap + WD].reshape(-1, C)
                    act_grad = act_grad + jnp.dot(later, kernel[time_tap, high_tap, wide_tap].T, preferred_element_type=jnp.float32)
                    window = act_pad[time_tap:time_tap + LFRAMES, high_tap:high_tap + HT, wide_tap:wide_tap + WD].reshape(-1, C)
                    conv_terms.append(jnp.dot(window.T, conv_grad, preferred_element_type=jnp.float32))
        norm_grad, = pullback(act_grad.reshape(LFRAMES, HT, WD, C))
        clip_out = (hidden_grad.reshape(LFRAMES, HT, WD, C) + norm_grad).astype(jnp.bfloat16)
        return ((totals[0] + jnp.concatenate(conv_terms, axis=0), totals[1] + jnp.concatenate(up_terms, axis=0)), clip_out)
    initial = (jnp.zeros((27 * C, C), jnp.float32), jnp.zeros((3 * C, 2 * C), jnp.float32))
    (conv_total, up_total), features_grad = lax.scan(per_crop, initial, (features, cotangent))
    scale = 1.0 / math.sqrt(POSITIONS)
    return (features_grad, conv_total * scale, up_total * scale)
```

```python
import functools
import math

import jax
import jax.numpy as jnp
from jax import lax
from jax.experimental import pallas as pl
from jax.experimental.pallas import tpu as pltpu
from jax.sharding import PartitionSpec as P

G = 32


EPSILON = 1e-06
LANES = 128


def from_behind(value, axis, steps):
    count = lax.axis_size(axis)
    first, last = (max(0, -steps), min(count, count - steps))
    return lax.ppermute(value, axis, [(source, source + steps) for source in range(first, last)])


def exchange(blocks, axis, kind):
    count = lax.axis_size(axis)
    me = lax.axis_index(axis)
    total = lax.dynamic_index_in_dim(blocks, me, 0, keepdims=False)
    for step in range(1, count):
        pairs = [(place, place ^ step) for place in range(count)]
        sent = lax.dynamic_index_in_dim(blocks, me ^ step, 0, keepdims=False).astype(kind)
        total = total + lax.ppermute(sent, axis, pairs).astype(jnp.float32)
    return total


def reduce_data(part):
    count = lax.axis_size("dp")
    me = lax.axis_index("dp")
    rows = part.shape[0] // count
    blocks = part.reshape((count // 2, 2, rows) + part.shape[1:])
    core = me % 2
    kept = lax.dynamic_index_in_dim(blocks, core, 1, keepdims=False)
    sent = lax.dynamic_index_in_dim(blocks, 1 - core, 1, keepdims=False)
    pair = kept + lax.ppermute(sent, "dp", [(place, place ^ 1) for place in range(count)])
    home = me // 2
    total = lax.dynamic_index_in_dim(pair, home, 0, keepdims=False)
    for step in range(1, count // 2):
        pairs = [(place, place ^ (2 * step)) for place in range(count)]
        piece = lax.dynamic_index_in_dim(pair, home ^ step, 0, keepdims=False)
        piece = lax.ppermute(piece.astype(jnp.bfloat16), "dp", pairs)
        total = total + piece.astype(jnp.float32)
    return total


def group_mean(field):
    crops, frames, height, breadth, channels = field.shape
    sums = jnp.sum(field, axis=(2, 3)).reshape(crops, frames, G, channels // G)
    means = jnp.sum(sums, axis=-1, keepdims=True) / (height * breadth * channels // G)
    spread = jnp.broadcast_to(means, sums.shape).reshape(crops, frames, channels)
    return spread[:, :, None, None, :]


def weight_body(frames, breadth, left_ref, right_ref, out_ref):
    high = 2 - pl.program_id(0) // 3
    wide = 2 - lax.rem(pl.program_id(0), 3)
    height, lanes = right_ref.shape[-2:]
    windows = [
        right_ref[high, 2 - tap : 2 - tap + frames, pl.ds(wide, breadth)].reshape(
            frames * breadth * height, lanes
        )
        for tap in range(3)
    ]
    product = jnp.dot(
        left_ref[...], jnp.concatenate(windows, axis=1), preferred_element_type=jnp.float32
    )
    for tap in range(3):
        out_ref[tap, 0] = product[:, tap * lanes : tap * lanes + out_ref.shape[-1]]


def weight_gradient(act_all, columns):
    frames, height, breadth, channels = act_all.shape
    width = columns.shape[-1]
    lanes = -(-width // LANES) * LANES
    left = act_all.transpose(3, 0, 2, 1).reshape(channels, -1)
    turned = jnp.pad(
        columns.transpose(0, 2, 1, 3), ((0, 2), (1, 1), (1, 1), (0, lanes - width))
    )
    right = jnp.stack([turned[:, :, high : high + height] for high in range(3)])
    positions = frames * height * breadth
    out = pl.pallas_call(
        functools.partial(weight_body, frames, breadth),
        grid=(9,),
        in_specs=[
            pl.BlockSpec(left.shape, lambda step: (0, 0)),
            pl.BlockSpec(right.shape, lambda step: (0, 0, 0, 0, 0)),
        ],
        out_specs=pl.BlockSpec((3, 1, channels, width), lambda step: (0, step, 0, 0)),
        out_shape=jax.ShapeDtypeStruct((3, 9, channels, width), jnp.float32),
        compiler_params=pltpu.CompilerParams(vmem_limit_bytes=48 * 1024 * 1024),
        cost_estimate=pl.CostEstimate(
            flops=54 * positions * channels * lanes,
            bytes_accessed=2 * (left.size + right.size) + 4 * 27 * channels * width,
            transcendentals=0,
        ),
    )(left, right)
    return out.reshape(27 * channels, width)


def shards(features, conv_weight, up_weight, cotangent):
    crop_count, frames, height, breadth, channels = features.shape
    data_count = lax.axis_size("dp")
    time_count = lax.axis_size("tm")
    scale = 1.0 / math.sqrt(crop_count * frames * height * breadth * data_count * time_count)
    kernel = conv_weight.reshape(3, 3, 3, channels, channels)
    me = lax.axis_index("tm")

    up_grad = jnp.concatenate([cotangent[:, 0::2], cotangent[:, 1::2]], axis=-1)
    taps = lax.dot_general(
        up_grad.reshape(-1, 2 * channels),
        up_weight,
        (((1,), (1,)), ((), ())),
        preferred_element_type=jnp.float32,
    ).reshape((crop_count, frames, height, breadth, 3 * channels))

    def share(frame):
        terms = [
            taps[:, frame + 2 - k, :, :, k * channels : (k + 1) * channels]
            for k in range(3)
            if 0 <= frame + 2 - k < frames
        ]
        return functools.reduce(jnp.add, terms)

    far = jnp.stack([share(-2), share(-1)], axis=1)
    before = from_behind(far.astype(jnp.bfloat16), "tm", -1)

    field = features.astype(jnp.float32)
    center = field - group_mean(field)
    inverse = lax.rsqrt(group_mean(center * center) + EPSILON)
    normed = center * inverse
    gate = 1.0 / (1.0 + jnp.exp(-normed))
    act = (normed * gate).astype(jnp.bfloat16)
    act_prior = from_behind(act[:, frames - 2 :], "tm", 1)

    hidden_grad = jnp.stack([share(frame) for frame in range(frames)], axis=1)
    hidden_grad = hidden_grad.at[:, frames - 2 :].add(before.astype(jnp.float32))
    conv_grad = hidden_grad.astype(jnp.bfloat16)
    conv_next = from_behind(conv_grad[:, :2], "tm", -1)

    width = channels // time_count
    gathered = (crop_count, time_count) + features.shape[1:]
    act_sent, _ = lax.optimization_barrier((act, before))
    act_all = lax.dynamic_update_slice(
        jnp.zeros(gathered, jnp.bfloat16), act[:, None], (0, me, 0, 0, 0, 0)
    )
    own = lax.dynamic_slice_in_dim(conv_grad, me * width, width, 4)
    conv_columns = lax.dynamic_update_slice(
        jnp.zeros(gathered[:-1] + (width,), jnp.bfloat16), own[:, None], (0, me, 0, 0, 0, 0)
    )
    for step in range(1, time_count):
        pairs = [(place, place ^ step) for place in range(time_count)]
        other = me ^ step
        piece = lax.dynamic_slice_in_dim(conv_grad, other * width, width, 4)
        piece = lax.ppermute(piece, "tm", pairs)
        conv_columns = lax.dynamic_update_slice(
            conv_columns, piece[:, None], (0, other, 0, 0, 0, 0)
        )
        block = lax.ppermute(act_sent, "tm", pairs)
        act_all = lax.dynamic_update_slice(act_all, block[:, None], (0, other, 0, 0, 0, 0))
    whole = (crop_count, time_count * frames, height, breadth)
    act_all = act_all.reshape(whole + (channels,))
    conv_columns = conv_columns.reshape(whole + (width,))

    conv_part = weight_gradient(act_all[0], conv_columns[0])
    for crop in range(1, crop_count):
        conv_part = conv_part + weight_gradient(act_all[crop], conv_columns[crop])

    conv_out = lax.conv_general_dilated(
        jnp.concatenate([act_prior, act], axis=1),
        kernel,
        (1, 1, 1),
        ((0, 0), (1, 1), (1, 1)),
        dimension_numbers=("NDHWC", "DHWIO", "NDHWC"),
        preferred_element_type=jnp.float32,
    )
    hidden = (field + conv_out).astype(jnp.bfloat16)
    hidden_prior = from_behind(hidden[:, frames - 2 :], "tm", 1)
    hidden_ext = jnp.concatenate([hidden_prior, hidden], axis=1)
    hidden_cols = jnp.concatenate([hidden_ext[:, k : k + frames] for k in range(3)], axis=-1)
    hidden_cols = hidden_cols.reshape(-1, 3 * channels)
    halves = [
        lax.dot_general(
            hidden_cols,
            cotangent[:, half::2].reshape(-1, channels),
            (((0,), (0,)), ((), ())),
            preferred_element_type=jnp.float32,
        )
        for half in range(2)
    ]
    conv_ext = jnp.concatenate([conv_grad, conv_next], axis=1)
    conv_ext, conv_part, up_part = lax.optimization_barrier(
        (conv_ext, conv_part, jnp.concatenate(halves, axis=1))
    )
    grad_conv = reduce_data(conv_part) * scale
    up_part = reduce_data(up_part)
    up_width = 2 * channels // time_count
    up_part = up_part.reshape(-1, time_count, up_width).transpose(1, 0, 2)
    grad_up = exchange(up_part, "tm", jnp.float32) * scale

    act_grad = lax.conv_general_dilated(
        conv_ext,
        lax.rev(kernel, (0, 1, 2)),
        (1, 1, 1),
        ((0, 0), (1, 1), (1, 1)),
        dimension_numbers=("NDHWC", "DHWOI", "NDHWC"),
        preferred_element_type=jnp.float32,
    )
    normed_grad = act_grad * gate * (1.0 + normed * (1.0 - gate))
    first = group_mean(normed_grad)
    second = group_mean(normed_grad * normed)
    norm_grad = inverse * (normed_grad - first - normed * second)
    features_grad = (hidden_grad + norm_grad).astype(jnp.bfloat16)
    return (features_grad, grad_conv, grad_up)


def solution(mesh):
    in_specs = (P("dp", "tm", None, None, None), P(), P(), P("dp", "tm", None, None, None))
    out_specs = (P("dp", "tm", None, None, None), P("dp", "tm"), P("dp", "tm"))
    return jax.shard_map(shards, mesh=mesh, in_specs=in_specs, out_specs=out_specs, check_vma=False)
```

```python
import functools
import math

import jax
import jax.numpy as jnp
from jax import lax
from jax.experimental import pallas as pl
from jax.experimental.pallas import tpu as pltpu
from jax.sharding import PartitionSpec as P

G = 32


EPSILON = 1e-06
LANES = 128


def from_behind(value, axis, steps):
    count = lax.axis_size(axis)
    first, last = (max(0, -steps), min(count, count - steps))
    return lax.ppermute(value, axis, [(source, source + steps) for source in range(first, last)])


def exchange(blocks, axis, kind):
    count = lax.axis_size(axis)
    me = lax.axis_index(axis)
    total = lax.dynamic_index_in_dim(blocks, me, 0, keepdims=False)
    for step in range(1, count):
        pairs = [(place, place ^ step) for place in range(count)]
        sent = lax.dynamic_index_in_dim(blocks, me ^ step, 0, keepdims=False).astype(kind)
        total = total + lax.ppermute(sent, axis, pairs).astype(jnp.float32)
    return total


def pair_sum(part):
    count = lax.axis_size("dp")
    me = lax.axis_index("dp")
    rows = part.shape[0] // count
    blocks = part.reshape((count // 2, 2, rows) + part.shape[1:])
    core = me % 2
    kept = lax.dynamic_index_in_dim(blocks, core, 1, keepdims=False)
    sent = lax.dynamic_index_in_dim(blocks, 1 - core, 1, keepdims=False)
    return kept + lax.ppermute(sent, "dp", [(place, place ^ 1) for place in range(count)])


def reduce_pairs(pair):
    count = lax.axis_size("dp")
    me = lax.axis_index("dp")
    home = me // 2
    total = lax.dynamic_index_in_dim(pair, home, 0, keepdims=False)
    for step in range(1, count // 2):
        pairs = [(place, place ^ (2 * step)) for place in range(count)]
        piece = lax.dynamic_index_in_dim(pair, home ^ step, 0, keepdims=False)
        piece = lax.ppermute(piece.astype(jnp.bfloat16), "dp", pairs)
        total = total + piece.astype(jnp.float32)
    return total


def group_mean(field):
    crops, frames, height, breadth, channels = field.shape
    sums = jnp.sum(field, axis=(2, 3)).reshape(crops, frames, G, channels // G)
    means = jnp.sum(sums, axis=-1, keepdims=True) / (height * breadth * channels // G)
    spread = jnp.broadcast_to(means, sums.shape).reshape(crops, frames, channels)
    return spread[:, :, None, None, :]


def weight_body(frames, breadth, left_ref, right_ref, out_ref):
    high = 2 - pl.program_id(0) // 3
    wide = 2 - lax.rem(pl.program_id(0), 3)
    height, lanes = right_ref.shape[-2:]
    windows = [
        right_ref[high, 2 - tap : 2 - tap + frames, pl.ds(wide, breadth)].reshape(
            frames * breadth * height, lanes
        )
        for tap in range(3)
    ]
    product = jnp.dot(
        left_ref[...], jnp.concatenate(windows, axis=1), preferred_element_type=jnp.float32
    )
    for tap in range(3):
        out_ref[tap, 0] = product[:, tap * lanes : tap * lanes + out_ref.shape[-1]]


def weight_gradient(act_all, columns):
    frames, height, breadth, channels = act_all.shape
    width = columns.shape[-1]
    lanes = -(-width // LANES) * LANES
    left = act_all.transpose(3, 0, 2, 1).reshape(channels, -1)
    turned = jnp.pad(
        columns.transpose(0, 2, 1, 3), ((0, 2), (1, 1), (1, 1), (0, lanes - width))
    )
    right = jnp.stack([turned[:, :, high : high + height] for high in range(3)])
    positions = frames * height * breadth
    out = pl.pallas_call(
        functools.partial(weight_body, frames, breadth),
        grid=(9,),
        in_specs=[
            pl.BlockSpec(left.shape, lambda step: (0, 0)),
            pl.BlockSpec(right.shape, lambda step: (0, 0, 0, 0, 0)),
        ],
        out_specs=pl.BlockSpec((3, 1, channels, width), lambda step: (0, step, 0, 0)),
        out_shape=jax.ShapeDtypeStruct((3, 9, channels, width), jnp.float32),
        compiler_params=pltpu.CompilerParams(vmem_limit_bytes=48 * 1024 * 1024),
        cost_estimate=pl.CostEstimate(
            flops=54 * positions * channels * lanes,
            bytes_accessed=2 * (left.size + right.size) + 4 * 27 * channels * width,
            transcendentals=0,
        ),
    )(left, right)
    return out.reshape(27 * channels, width)


def shards(features, conv_weight, up_weight, cotangent):
    crop_count, frames, height, breadth, channels = features.shape
    data_count = lax.axis_size("dp")
    time_count = lax.axis_size("tm")
    scale = 1.0 / math.sqrt(crop_count * frames * height * breadth * data_count * time_count)
    kernel = conv_weight.reshape(3, 3, 3, channels, channels)
    me = lax.axis_index("tm")

    up_grad = jnp.concatenate([cotangent[:, 0::2], cotangent[:, 1::2]], axis=-1)
    taps = lax.dot_general(
        up_grad.reshape(-1, 2 * channels),
        up_weight,
        (((1,), (1,)), ((), ())),
        preferred_element_type=jnp.float32,
    ).reshape((crop_count, frames, height, breadth, 3 * channels))

    def share(frame):
        terms = [
            taps[:, frame + 2 - k, :, :, k * channels : (k + 1) * channels]
            for k in range(3)
            if 0 <= frame + 2 - k < frames
        ]
        return functools.reduce(jnp.add, terms)

    far = jnp.stack([share(-2), share(-1)], axis=1)
    before = from_behind(far.astype(jnp.bfloat16), "tm", -1)

    field = features.astype(jnp.float32)
    center = field - group_mean(field)
    inverse = lax.rsqrt(group_mean(center * center) + EPSILON)
    normed = center * inverse
    gate = 1.0 / (1.0 + jnp.exp(-normed))
    act = (normed * gate).astype(jnp.bfloat16)
    act_prior = from_behind(act[:, frames - 2 :], "tm", 1)

    hidden_grad = jnp.stack([share(frame) for frame in range(frames)], axis=1)
    hidden_grad = hidden_grad.at[:, frames - 2 :].add(before.astype(jnp.float32))
    conv_grad = hidden_grad.astype(jnp.bfloat16)
    conv_next = from_behind(conv_grad[:, :2], "tm", -1)

    width = channels // time_count
    gathered = (crop_count, time_count) + features.shape[1:]
    act_sent, _ = lax.optimization_barrier((act, before))
    act_all = lax.dynamic_update_slice(
        jnp.zeros(gathered, jnp.bfloat16), act[:, None], (0, me, 0, 0, 0, 0)
    )
    own = lax.dynamic_slice_in_dim(conv_grad, me * width, width, 4)
    conv_columns = lax.dynamic_update_slice(
        jnp.zeros(gathered[:-1] + (width,), jnp.bfloat16), own[:, None], (0, me, 0, 0, 0, 0)
    )
    for step in range(1, time_count):
        pairs = [(place, place ^ step) for place in range(time_count)]
        other = me ^ step
        piece = lax.dynamic_slice_in_dim(conv_grad, other * width, width, 4)
        piece = lax.ppermute(piece, "tm", pairs)
        conv_columns = lax.dynamic_update_slice(
            conv_columns, piece[:, None], (0, other, 0, 0, 0, 0)
        )
        block = lax.ppermute(act_sent, "tm", pairs)
        act_all = lax.dynamic_update_slice(act_all, block[:, None], (0, other, 0, 0, 0, 0))
    whole = (crop_count, time_count * frames, height, breadth)
    act_all = act_all.reshape(whole + (channels,))
    conv_columns = conv_columns.reshape(whole + (width,))

    conv_part = weight_gradient(act_all[0], conv_columns[0])
    for crop in range(1, crop_count):
        conv_part = conv_part + weight_gradient(act_all[crop], conv_columns[crop])

    conv_out = lax.conv_general_dilated(
        jnp.concatenate([act_prior, act], axis=1),
        kernel,
        (1, 1, 1),
        ((0, 0), (1, 1), (1, 1)),
        dimension_numbers=("NDHWC", "DHWIO", "NDHWC"),
        preferred_element_type=jnp.float32,
    )
    hidden = (field + conv_out).astype(jnp.bfloat16)
    hidden_prior = from_behind(hidden[:, frames - 2 :], "tm", 1)
    hidden_ext = jnp.concatenate([hidden_prior, hidden], axis=1)
    hidden_cols = jnp.concatenate([hidden_ext[:, k : k + frames] for k in range(3)], axis=-1)
    hidden_cols = hidden_cols.reshape(-1, 3 * channels)
    halves = [
        lax.dot_general(
            hidden_cols,
            cotangent[:, half::2].reshape(-1, channels),
            (((0,), (0,)), ((), ())),
            preferred_element_type=jnp.float32,
        )
        for half in range(2)
    ]
    conv_ext = jnp.concatenate([conv_grad, conv_next], axis=1)
    conv_ext, conv_part, up_part = lax.optimization_barrier(
        (conv_ext, pair_sum(conv_part), pair_sum(jnp.concatenate(halves, axis=1)))
    )
    grad_conv = reduce_pairs(conv_part) * scale
    up_part = reduce_pairs(up_part)
    up_width = 2 * channels // time_count
    up_part = up_part.reshape(-1, time_count, up_width).transpose(1, 0, 2)
    grad_up = exchange(up_part, "tm", jnp.float32) * scale

    act_grad = lax.conv_general_dilated(
        conv_ext,
        lax.rev(kernel, (0, 1, 2)),
        (1, 1, 1),
        ((0, 0), (1, 1), (1, 1)),
        dimension_numbers=("NDHWC", "DHWOI", "NDHWC"),
        preferred_element_type=jnp.float32,
    )
    normed_grad = act_grad * gate * (1.0 + normed * (1.0 - gate))
    first = group_mean(normed_grad)
    second = group_mean(normed_grad * normed)
    norm_grad = inverse * (normed_grad - first - normed * second)
    features_grad = (hidden_grad + norm_grad).astype(jnp.bfloat16)
    return (features_grad, grad_conv, grad_up)


def solution(mesh):
    in_specs = (P("dp", "tm", None, None, None), P(), P(), P("dp", "tm", None, None, None))
    out_specs = (P("dp", "tm", None, None, None), P("dp", "tm"), P("dp", "tm"))
    return jax.shard_map(shards, mesh=mesh, in_specs=in_specs, out_specs=out_specs, check_vma=False)
```
